32 devices in a mesh: gx: 8 (over y, x, core), ga: 4 (over z).
Axes of the slice: x: 2, y: 2, z: 4, core: 2. Of those that a mesh axis runs over, the one named last changes fastest.
Arguments:
- velocity: float32 [3, 32, 384, 768], P(None, 'gx', 'ga'), may hold values from -6 to 6
- accumulated: float32 [3, 32, 384, 768], P(None, 'gx', 'ga'), may hold values from -6 to 6
- wall_first: float32 [384, 384], replicated, may hold values from -0.3125 to 0.3125
- wall_second: float32 [384, 384], replicated, may hold values from -0.3125 to 0.3125
- recycle_rows: int32 [384], replicated, may hold values from 0 to 382
- weight_index: int32 [384], replicated, may hold values from 0 to 63
- weight_table: float32 [64], replicated, may hold values from 0 to 1
Outputs:
- velocity_next: float32 [3, 32, 384, 768], P(None, 'gx', 'ga')
- accumulated_next: float32 [3, 32, 384, 768], P(None, 'gx', 'ga')
The draws below stay inside these ranges and needn't reach their ends.
Inputs may be any that keep to these rules, and one draw needn't show every extreme that they name: `recycle_rows`: each entry names the lower of two adjacent recycle-plane rows. `weight_index`: each entry names one entry of weight_table.
All inputs are finite; a program needn't handle non-finite values.
Results may differ from the reference program's by a relative error of at most 0.0001.
Values sent between devices are 32-bit elements; how exact they have to be, the bound alone decides.
A program may use at most 128 MiB of HBM per device.

```python
import math
import jax
import jax.numpy as jnp
from jax import lax

NY = 384
NZ = 768
CX = 4
HALO = 4
NW = 64
NX = 32
RECYCLE_SLAB = 7


def place_ends(entries, own_key, least, largest):
    place = [jax.random.randint(jax.random.fold_in(own_key, axis), (), 0, length) for axis, length in enumerate(entries.shape)]
    widest = entries.shape.index(max(entries.shape))
    next_to = place[:widest] + [(place[widest] + 1) % entries.shape[widest]] + place[widest + 1:]
    return entries.at[tuple(place)].set(least).at[tuple(next_to)].set(largest)


def steps_of(stream_key, shape, split, least, largest):
    def one(position, parts):
        heights = jax.random.uniform(jax.random.fold_in(jax.random.fold_in(stream_key, 6), position), (parts,), jnp.float32, least / len(split), largest / len(split))
        return jnp.repeat(jnp.exp(heights), shape[position] // parts).reshape((-1,) + (1,) * (len(shape) - position - 1))

    factor_of = one(*split[0])
    for cut in split[1:]:
        factor_of = factor_of * one(*cut)
    return factor_of


def bell_draw(key, shape, deviation, most, pieces=(), held_as=jnp.bfloat16):
    result = deviation * jax.random.normal(key, shape, jnp.float32)
    if pieces:
        result = result * steps_of(key, shape, pieces, -0.22, 0.18)
    return jnp.clip(result, -most, most).astype(held_as)


def setup_inputs(seed: int = 0) -> dict:
    seeds = jax.random.split(jax.random.key(seed), 8)
    return {
        "velocity": bell_draw(seeds[0], (3, NX, NY, NZ), 1.0, 6.0, ((1, 8), (2, 4)), jnp.float32),
        "accumulated": bell_draw(seeds[1], (3, NX, NY, NZ), 1.0, 6.0, ((1, 8), (2, 4)), jnp.float32),
        "wall_first": bell_draw(seeds[2], (NY, NY), NY ** -0.5, 0.3125, (), jnp.float32),
        "wall_second": bell_draw(seeds[3], (NY, NY), NY ** -0.5, 0.3125, (), jnp.float32),
        "recycle_rows": place_ends(jax.random.randint(seeds[4], (NY,), 0, NY - 1), jax.random.fold_in(seeds[4], 1), 0, (NY - 1) - 1).astype(jnp.int32),
        "weight_index": place_ends(jax.random.randint(seeds[5], (NY,), 0, NW), jax.random.fold_in(seeds[5], 1), 0, NW - 1).astype(jnp.int32),
        "weight_table": jnp.clip(jax.random.uniform(seeds[6], (NW,), jnp.float32, 0.0, 1.0), 0.0, 1.0),
    }


first_coef = (0.8, -0.2, 4.0 / 105.0, -1.0 / 280.0)
second_coef = (1.6, -0.2, 8.0 / 315.0, -1.0 / 560.0)
center_coef = -205.0 / 72.0
step_size = 0.2
viscosity = 0.2
keep_rate = -5.0 / 9.0
update_rate = 15.0 / 16.0


def streamwise(field, inflow):
    lower = jnp.broadcast_to(inflow[None], (HALO, NY, NZ))
    upper = jnp.broadcast_to(field[-1:], (HALO, NY, NZ))
    padded = jnp.concatenate([lower, field, upper], 0)
    first = jnp.zeros_like(field)
    second = center_coef * field
    for offset in range(1, HALO + 1):
        ahead = padded[HALO + offset:HALO + offset + NX]
        behind = padded[HALO - offset:HALO - offset + NX]
        first = first + first_coef[offset - 1] * (ahead - behind)
        second = second + second_coef[offset - 1] * (ahead + behind)
    return first, second


def spanwise(field):
    spectrum = jnp.fft.rfft(field, axis=-1)
    levels = jnp.arange(NZ // 2 + 1)
    waves = 2.0 * math.pi * levels / NZ
    odd_waves = jnp.where(levels == NZ // 2, 0.0, waves)
    first = jnp.fft.irfft(1j * odd_waves * spectrum, n=NZ, axis=-1)
    second = jnp.fft.irfft(-(waves * waves) * spectrum, n=NZ, axis=-1)
    return first.astype(field.dtype), second.astype(field.dtype)


def reference(velocity, accumulated, wall_first, wall_second, recycle_rows, weight_index, weight_table):
    recycle = velocity[:, RECYCLE_SLAB * CX]
    frac = weight_table[weight_index][None, :, None]
    inflow = (1.0 - frac) * recycle[:, recycle_rows] + frac * recycle[:, recycle_rows + 1]
    outputs_new = []
    outputs_acc = []
    for component in range(3):
        field = velocity[component]
        stream_first, stream_second = streamwise(field, inflow[component])
        normal_first = jnp.einsum('ij,xjz->xiz', wall_first, field, precision=lax.Precision.HIGHEST)
        normal_second = jnp.einsum('ij,xjz->xiz', wall_second, field, precision=lax.Precision.HIGHEST)
        span_first, span_second = spanwise(field)
        tendency = -(velocity[0] * stream_first + velocity[1] * normal_first + velocity[2] * span_first) + viscosity * (stream_second + normal_second + span_second)
        acc_next = keep_rate * accumulated[component] + step_size * tendency
        outputs_acc.append(acc_next)
        outputs_new.append(field + update_rate * acc_next)
    return jnp.stack(outputs_new), jnp.stack(outputs_acc)
```

```python
import functools
import math

import jax
import jax.numpy as jnp
import numpy as np
from jax import lax
from jax.experimental import pallas as pl
from jax.experimental.pallas import tpu as pltpu
from jax.sharding import PartitionSpec as P

HALO = 4


first_coef = (0.8, -0.2, 4.0 / 105.0, -1.0 / 280.0)
second_coef = (1.6, -0.2, 8.0 / 315.0, -1.0 / 560.0)
center_coef = -205.0 / 72.0
step_size = 0.2
viscosity = 0.2
keep_rate = -5.0 / 9.0
update_rate = 15.0 / 16.0


def padded_2(cells, sides, width):
    for axis, dim in sides:
        count = lax.axis_size(axis)
        ends = count - 1
        head = lax.slice_in_dim(cells, 0, width, axis=dim)
        tail = lax.slice_in_dim(cells, cells.shape[dim] - width, cells.shape[dim], axis=dim)
        cells = jnp.concatenate(
            [
                lax.ppermute(tail, axis, [(i, (i + 1) % count) for i in range(ends)]),
                cells,
                lax.ppermute(head, axis, [((i + 1) % count, i) for i in range(ends)]),
            ],
            axis=dim,
        )
    return cells


def passed_along(shard, axis, by):
    peers = lax.axis_size(axis)
    pairs = [(i, i + by) for i in range(peers) if 0 <= i + by < peers]
    return lax.ppermute(shard, axis, pairs)


def spanwise_table(length):
    places = jnp.arange(length, dtype=jnp.int32)
    apart = places[None, :] - places[:, None]
    apart = jnp.remainder(apart + length // 2, length) - length // 2
    parity = 1.0 - 2.0 * jnp.remainder(apart, 2).astype(jnp.float32)
    spacing = 2.0 * math.pi / length
    angle = apart.astype(jnp.float32) * (0.5 * spacing)
    same = apart == 0
    safe_sine = jnp.where(same, 1.0, jnp.sin(angle))
    first = jnp.where(same, 0.0, 0.5 * spacing * parity * jnp.cos(angle) / safe_sine)
    second = jnp.where(
        same,
        -math.pi * math.pi / 3.0 - spacing * spacing / 6.0,
        -0.5 * spacing * spacing * parity / (safe_sine * safe_sine),
    )
    return jnp.concatenate([first, second], 1)


def streamwise(field, inflow):
    extent = field.shape[1]
    padded = padded_2(field, (("gx", 1),), HALO)
    at_inlet = lax.axis_index("gx") == 0
    at_outlet = lax.axis_index("gx") == lax.axis_size("gx") - 1
    ghost_shape = (field.shape[0], HALO) + field.shape[2:]
    lower = jnp.where(at_inlet, jnp.broadcast_to(inflow[:, None], ghost_shape), padded[:, :HALO])
    upper = jnp.where(
        at_outlet, jnp.broadcast_to(field[:, -1:], ghost_shape), padded[:, HALO + extent :]
    )
    padded = jnp.concatenate([lower, field, upper], 1)
    first = jnp.zeros_like(field)
    second = center_coef * field
    for offset in range(1, HALO + 1):
        ahead = padded[:, HALO + offset : HALO + offset + extent]
        behind = padded[:, HALO - offset : HALO - offset + extent]
        first = first + first_coef[offset - 1] * (ahead - behind)
        second = second + second_coef[offset - 1] * (ahead + behind)
    return -(field[0:1] * first) + viscosity * second


def wall_terms(columns, wall_first, wall_second):
    first = jnp.einsum(
        "ij,cxjz->cxiz",
        wall_first,
        columns,
        precision=lax.Precision.HIGHEST,
        preferred_element_type=jnp.float32,
    )
    second = jnp.einsum(
        "ij,cxjz->cxiz",
        wall_second,
        columns,
        precision=lax.Precision.HIGHEST,
        preferred_element_type=jnp.float32,
    )
    return -(columns[1:2] * first) + viscosity * second


def interpolation(rows, picks, weight_table, height):
    levels = jnp.arange(weight_table.shape[0], dtype=jnp.int32)
    frac = jnp.sum(
        jnp.where(picks[:, None] == levels[None, :], weight_table[None, :], 0.0), axis=1
    )[:, None]
    apart = jnp.arange(height, dtype=jnp.int32)[None, :] - rows[:, None]
    return jnp.where(apart == 0, 1.0 - frac, jnp.where(apart == 1, frac, 0.0))


def rescale(plane, rows, picks, weight_table):
    return jnp.einsum(
        "ij,cjz->ciz",
        interpolation(rows, picks, weight_table, plane.shape[1]),
        plane,
        precision=lax.Precision.HIGHEST,
        preferred_element_type=jnp.float32,
    )


def fetch_recycle(plane):
    count = lax.axis_size("gx")
    return passed_along(plane, "gx", 1 - count)


def shards(
    velocity, accumulated, wall_first, wall_second, recycle_rows, weight_index, weight_table
):
    span = velocity.shape[3]
    rows_here = velocity.shape[2]
    lines = velocity.reshape(-1, span)
    derived = jnp.dot(
        lines,
        spanwise_table(span),
        precision=lax.Precision.HIGHEST,
        preferred_element_type=jnp.float32,
    )
    span_first = derived[:, :span].reshape(velocity.shape)
    span_second = derived[:, span:].reshape(velocity.shape)
    tendency = -(velocity[2:3] * span_first) + viscosity * span_second
    arrived = fetch_recycle(velocity[:, 0])
    whole_plane = lax.all_gather(arrived, "ga", axis=1, tiled=True)
    start = lax.axis_index("ga") * rows_here
    rows = lax.dynamic_slice_in_dim(recycle_rows, start, rows_here)
    picks = lax.dynamic_slice_in_dim(weight_index, start, rows_here)
    inflow = rescale(whole_plane, rows, picks, weight_table)
    tendency = tendency + streamwise(velocity, inflow)
    tendency = tendency + lax.all_to_all(
        wall_terms(
            lax.all_to_all(velocity, "ga", split_axis=3, concat_axis=2, tiled=True),
            wall_first,
            wall_second,
        ),
        "ga",
        split_axis=2,
        concat_axis=3,
        tiled=True,
    )
    accumulated_next = keep_rate * accumulated + step_size * tendency
    return (velocity + update_rate * accumulated_next, accumulated_next)


MESH = pl.DeviceIdType.MESH
PARTS = 3


def folded_tables(length):
    half = length // 2
    apart = np.arange(length)[None, :] - np.arange(length)[:, None]
    apart = np.remainder(apart + half, length) - half
    parity = 1.0 - 2.0 * np.remainder(apart, 2)
    spacing = 2.0 * math.pi / length
    angle = apart * (0.5 * spacing)
    same = apart == 0
    sine = np.where(same, 1.0, np.sin(angle))
    first = np.where(same, 0.0, 0.5 * spacing * parity * np.cos(angle) / sine)
    first = np.where(np.abs(apart) == half, 0.0, first)
    second = np.where(
        same,
        -math.pi * math.pi / 3.0 - spacing * spacing / 6.0,
        -0.5 * spacing * spacing * parity / (sine * sine),
    )
    near = np.concatenate([first[:half, :half], second[:half, :half]], 1)
    far = np.concatenate([first[half:, :half], second[half:, :half]], 1)
    return (
        (0.5 * (near + far)).astype(np.float32),
        (0.5 * (near - far)).astype(np.float32),
    )


def exact_dot(left, right):
    return jnp.dot(
        left, right, precision=lax.Precision.HIGHEST, preferred_element_type=jnp.float32
    )


def section_kernel(
    slabs,
    group,
    vel,
    acc,
    wall,
    mix,
    even,
    odd,
    vel_out,
    acc_out,
    gath,
    ret_src,
    ret_in,
    tend,
    lo,
    hi,
    inf_src,
    fwd_send,
    fwd_recv,
    ret_send,
    ret_recv,
    lo_send,
    lo_recv,
    hi_send,
    hi_recv,
    inf_send,
    inf_recv,
):
    gx = lax.axis_index("gx")
    me = lax.axis_index("ga")
    planes, rows, span = vel.shape[1:]
    width = span // PARTS
    half = span // 2
    height = group * rows
    chunks = 3 * PARTS
    not_first = gx > 0
    not_last = gx < slabs - 1
    source = jnp.logical_and(gx == slabs - 1, me == 0)

    def place(t):
        turn = t // PARTS
        c = lax.rem(1 + 2 * turn, 3)
        lanes = pl.ds(pl.multiple_of((t - turn * PARTS) * width, width), width)
        return c, lanes

    def fwd(t, d):
        c, lanes = place(t)
        peer = lax.rem(me + d, group)
        return pltpu.make_async_remote_copy(
            src_ref=vel.at[c, peer, :, lanes],
            dst_ref=gath.at[c, me, :, lanes],
            send_sem=fwd_send.at[t, d - 1],
            recv_sem=fwd_recv.at[t, d - 1],
            device_id={"ga": peer},
            device_id_type=MESH,
        )

    def ret(t, d):
        c, lanes = place(t)
        peer = lax.rem(me + d, group)
        return pltpu.make_async_remote_copy(
            src_ref=ret_src.at[c, peer, :, lanes],
            dst_ref=ret_in.at[c, me, :, lanes],
            send_sem=ret_send.at[t, d - 1],
            recv_sem=ret_recv.at[t, d - 1],
            device_id={"ga": peer},
            device_id_type=MESH,
        )

    def inf(t, k):
        c, lanes = place(t)
        return pltpu.make_async_remote_copy(
            src_ref=inf_src.at[c, k, :, lanes],
            dst_ref=lo.at[c, 0, :, lanes],
            send_sem=inf_send.at[t, k],
            recv_sem=inf_recv.at[t],
            device_id={"gx": 0, "ga": k},
            device_id_type=MESH,
        )

    def upward(c):
        return pltpu.make_async_remote_copy(
            src_ref=vel.at[c],
            dst_ref=lo.at[c],
            send_sem=lo_send.at[c],
            recv_sem=lo_recv.at[c],
            device_id={"gx": lax.rem(gx + 1, slabs)},
            device_id_type=MESH,
        )

    def downward(c):
        return pltpu.make_async_remote_copy(
            src_ref=vel.at[c],
            dst_ref=hi.at[c],
            send_sem=hi_send.at[c],
            recv_sem=hi_recv.at[c],
            device_id={"gx": lax.rem(gx + slabs - 1, slabs)},
            device_id_type=MESH,
        )

    barrier = pltpu.get_barrier_semaphore()
    for d in range(1, group):
        pl.semaphore_signal(
            barrier, inc=1, device_id={"ga": lax.rem(me + d, group)}, device_id_type=MESH
        )

    @pl.when(not_first)
    def _():
        pl.semaphore_signal(barrier, inc=1, device_id={"gx": gx - 1}, device_id_type=MESH)

    @pl.when(not_last)
    def _():
        pl.semaphore_signal(barrier, inc=1, device_id={"gx": gx + 1}, device_id_type=MESH)

    @pl.when(gx == 0)
    def _():
        pl.semaphore_signal(
            barrier, inc=1, device_id={"gx": slabs - 1, "ga": 0}, device_id_type=MESH
        )

    @pl.when(source)
    def _():
        for k in range(group):
            pl.semaphore_signal(
                barrier, inc=1, device_id={"gx": 0, "ga": k}, device_id_type=MESH
            )

    expected = (
        group
        - 1
        + not_first.astype(jnp.int32)
        + not_last.astype(jnp.int32)
        + (gx == 0).astype(jnp.int32)
        + group * source.astype(jnp.int32)
    )
    pl.semaphore_wait(barrier, expected)

    def send_fwd(t, carry):
        for d in range(1, group):
            fwd(t, d).start()
        return carry

    lax.fori_loop(0, PARTS, send_fwd, 0)
    for c in range(3):

        @pl.when(not_last)
        def _():
            upward(c).start()

        @pl.when(not_first)
        def _():
            downward(c).start()

    lax.fori_loop(PARTS, chunks, send_fwd, 0)

    for c in range(3):
        gath[c, me] = vel[c, me]

    @pl.when(jnp.logical_not(not_last))
    def _():
        for c in range(3):
            hi[c, 0] = vel[c, planes - 1]

    def spanwise_step(c, carry):
        left = vel[c, :, :, :half].reshape(planes * rows, half)
        right = vel[c, :, :, half:].reshape(planes * rows, half)
        sums = exact_dot(left + right, even[...])
        differences = exact_dot(left - right, odd[...])
        for side in range(2):
            both = sums + differences if side == 0 else sums - differences
            lanes = slice(side * half, (side + 1) * half)
            first = both[:, :half].reshape(planes, rows, half)
            second = both[:, half:].reshape(planes, rows, half)
            tend[c, :, :, lanes] = viscosity * second - vel[2, :, :, lanes] * first
        return carry

    lax.fori_loop(0, 3, spanwise_step, 0)

    def wall_step(t, carry):
        c, lanes = place(t)
        for d in range(1, group):
            fwd(t, d).wait_recv()
        columns = gath[c, :, :, lanes].reshape(height, width)
        normal = gath[1, :, :, lanes].reshape(height, width)
        both = exact_dot(wall[...], columns)
        term = viscosity * both[height:] - normal * both[:height]
        ret_src[c, :, :, lanes] = term.reshape(group, rows, width)
        for d in range(1, group):
            ret(t, d).start()
        ret_in[c, me, :, lanes] = ret_src[c, me, :, lanes]

        @pl.when(source)
        def _():
            mixed = exact_dot(mix[...], columns)
            inf_src[c, :, :, lanes] = mixed.reshape(group, rows, width)
            for k in range(group):
                inf(t, k).start()

        return carry

    lax.fori_loop(0, chunks, wall_step, 0)

    def stream_step(turn, carry):
        c = lax.rem(1 + 2 * turn, 3)

        @pl.when(not_first)
        def _():
            upward(c).wait_recv()

        @pl.when(gx == 0)
        def _():
            for part in range(PARTS):
                inf(turn * PARTS + part, 0).wait_recv()

        @pl.when(not_last)
        def _():
            downward(c).wait_recv()

        def tile(i, inner):
            block = i // PARTS
            where = pl.ds(pl.multiple_of(block * 8, 8), 8)
            lanes = pl.ds(pl.multiple_of((i - block * PARTS) * width, width), width)
            line = [
                lo[c, p * not_first.astype(jnp.int32), where, lanes] for p in range(HALO)
            ]
            line += [vel[c, p, where, lanes] for p in range(planes)]
            line += [hi[c, p * not_last.astype(jnp.int32), where, lanes] for p in range(HALO)]
            for x in range(planes):
                middle = x + HALO
                first = None
                second = center_coef * line[middle]
                for m in range(1, HALO + 1):
                    ahead, behind = line[middle + m], line[middle - m]
                    step = first_coef[m - 1] * (ahead - behind)
                    first = step if first is None else first + step
                    second = second + second_coef[m - 1] * (ahead + behind)
                total = viscosity * second - vel[0, x, where, lanes] * first
                tend[c, x, where, lanes] = tend[c, x, where, lanes] + total
            return inner

        lax.fori_loop(0, rows // 8 * PARTS, tile, 0)
        return carry

    lax.fori_loop(0, 3, stream_step, 0)

    def last_step(t, carry):
        c, lanes = place(t)
        for d in range(1, group):
            ret(t, d).wait_recv()
        tendency = tend[c, :, :, lanes] + ret_in[c, :, :, lanes]
        following = keep_rate * acc[c, :, :, lanes] + step_size * tendency
        acc_out[c, :, :, lanes] = following
        vel_out[c, :, :, lanes] = vel[c, :, :, lanes] + update_rate * following
        return carry

    lax.fori_loop(0, chunks, last_step, 0)

    def drain(t, carry):
        for d in range(1, group):
            fwd(t, d).wait_send()
            ret(t, d).wait_send()

        @pl.when(source)
        def _():
            for k in range(group):
                inf(t, k).wait_send()

        return carry

    lax.fori_loop(0, chunks, drain, 0)
    for c in range(3):

        @pl.when(not_last)
        def _():
            upward(c).wait_send()

        @pl.when(not_first)
        def _():
            downward(c).wait_send()


def fast_shards(
    slabs,
    group,
    velocity,
    accumulated,
    wall_first,
    wall_second,
    recycle_rows,
    weight_index,
    weight_table,
):
    _, planes, rows, span = velocity.shape
    height = rows * group
    chunks = 3 * PARTS
    even, odd = folded_tables(span)
    wall = jnp.concatenate([wall_first, wall_second], 0)
    mix = interpolation(recycle_rows, weight_index, weight_table, height)
    whole = pl.BlockSpec(memory_space=pltpu.VMEM)
    shape = jax.ShapeDtypeStruct(velocity.shape, jnp.float32)
    dma = pltpu.SemaphoreType.DMA
    slab = pltpu.VMEM((3, planes, rows, span), jnp.float32)
    exchanged = pltpu.VMEM((3, group, rows, span), jnp.float32)
    halo = pltpu.VMEM((3, HALO, rows, span), jnp.float32)
    return pl.pallas_call(
        functools.partial(section_kernel, slabs, group),
        out_shape=(shape, shape),
        in_specs=[whole] * 6,
        out_specs=(whole, whole),
        scratch_shapes=[
            exchanged,
            exchanged,
            slab,
            slab,
            halo,
            halo,
            exchanged,
            dma((chunks, group - 1)),
            dma((chunks, group - 1)),
            dma((chunks, group - 1)),
            dma((chunks, group - 1)),
            dma((3,)),
            dma((3,)),
            dma((3,)),
            dma((3,)),
            dma((chunks, group)),
            dma((chunks,)),
        ],
        compiler_params=pltpu.CompilerParams(
            collective_id=0, has_side_effects=True, vmem_limit_bytes=60 * 1024 * 1024
        ),
    )(velocity, accumulated, wall, mix, jnp.asarray(even), jnp.asarray(odd))


def solution(mesh):
    in_specs = (P(None, "gx", "ga", None), P(None, "gx", "ga", None), P(), P(), P(), P(), P())
    out_specs = (P(None, "gx", "ga", None), P(None, "gx", "ga", None))
    slabs, group = mesh.shape["gx"], mesh.shape["ga"]

    def body(velocity, *others):
        _, planes, rows, span = velocity.shape
        if planes == HALO == group and slabs > 2 and rows % 8 == 0 and span % 768 == 0:
            return fast_shards(slabs, group, velocity, *others)
        return shards(velocity, *others)

    return jax.shard_map(body, mesh=mesh, in_specs=in_specs, out_specs=out_specs, check_vma=False)
```

```python
import functools
import math

import jax
import jax.numpy as jnp
import numpy as np
from jax import lax
from jax.experimental import pallas as pl
from jax.experimental.pallas import tpu as pltpu
from jax.sharding import PartitionSpec as P

HALO = 4


first_coef = (0.8, -0.2, 4.0 / 105.0, -1.0 / 280.0)
second_coef = (1.6, -0.2, 8.0 / 315.0, -1.0 / 560.0)
center_coef = -205.0 / 72.0
step_size = 0.2
viscosity = 0.2
keep_rate = -5.0 / 9.0
update_rate = 15.0 / 16.0


def padded_2(cells, sides, width):
    for axis, dim in sides:
        count = lax.axis_size(axis)
        ends = count - 1
        head = lax.slice_in_dim(cells, 0, width, axis=dim)
        tail = lax.slice_in_dim(cells, cells.shape[dim] - width, cells.shape[dim], axis=dim)
        cells = jnp.concatenate(
            [
                lax.ppermute(tail, axis, [(i, (i + 1) % count) for i in range(ends)]),
                cells,
                lax.ppermute(head, axis, [((i + 1) % count, i) for i in range(ends)]),
            ],
            axis=dim,
        )
    return cells


def passed_along(shard, axis, by):
    peers = lax.axis_size(axis)
    pairs = [(i, i + by) for i in range(peers) if 0 <= i + by < peers]
    return lax.ppermute(shard, axis, pairs)


def spanwise_table(length):
    places = jnp.arange(length, dtype=jnp.int32)
    apart = places[None, :] - places[:, None]
    apart = jnp.remainder(apart + length // 2, length) - length // 2
    parity = 1.0 - 2.0 * jnp.remainder(apart, 2).astype(jnp.float32)
    spacing = 2.0 * math.pi / length
    angle = apart.astype(jnp.float32) * (0.5 * spacing)
    same = apart == 0
    safe_sine = jnp.where(same, 1.0, jnp.sin(angle))
    first = jnp.where(same, 0.0, 0.5 * spacing * parity * jnp.cos(angle) / safe_sine)
    second = jnp.where(
        same,
        -math.pi * math.pi / 3.0 - spacing * spacing / 6.0,
        -0.5 * spacing * spacing * parity / (safe_sine * safe_sine),
    )
    return jnp.concatenate([first, second], 1)


def streamwise(field, inflow):
    extent = field.shape[1]
    padded = padded_2(field, (("gx", 1),), HALO)
    at_inlet = lax.axis_index("gx") == 0
    at_outlet = lax.axis_index("gx") == lax.axis_size("gx") - 1
    ghost_shape = (field.shape[0], HALO) + field.shape[2:]
    lower = jnp.where(at_inlet, jnp.broadcast_to(inflow[:, None], ghost_shape), padded[:, :HALO])
    upper = jnp.where(
        at_outlet, jnp.broadcast_to(field[:, -1:], ghost_shape), padded[:, HALO + extent :]
    )
    padded = jnp.concatenate([lower, field, upper], 1)
    first = jnp.zeros_like(field)
    second = center_coef * field
    for offset in range(1, HALO + 1):
        ahead = padded[:, HALO + offset : HALO + offset + extent]
        behind = padded[:, HALO - offset : HALO - offset + extent]
        first = first + first_coef[offset - 1] * (ahead - behind)
        second = second + second_coef[offset - 1] * (ahead + behind)
    return -(field[0:1] * first) + viscosity * second


def wall_terms(columns, wall_first, wall_second):
    first = jnp.einsum(
        "ij,cxjz->cxiz",
        wall_first,
        columns,
        precision=lax.Precision.HIGHEST,
        preferred_element_type=jnp.float32,
    )
    second = jnp.einsum(
        "ij,cxjz->cxiz",
        wall_second,
        columns,
        precision=lax.Precision.HIGHEST,
        preferred_element_type=jnp.float32,
    )
    return -(columns[1:2] * first) + viscosity * second


def interpolation(rows, picks, weight_table, height):
    levels = jnp.arange(weight_table.shape[0], dtype=jnp.int32)
    frac = jnp.sum(
        jnp.where(picks[:, None] == levels[None, :], weight_table[None, :], 0.0), axis=1
    )[:, None]
    apart = jnp.arange(height, dtype=jnp.int32)[None, :] - rows[:, None]
    return jnp.where(apart == 0, 1.0 - frac, jnp.where(apart == 1, frac, 0.0))


def rescale(plane, rows, picks, weight_table):
    return jnp.einsum(
        "ij,cjz->ciz",
        interpolation(rows, picks, weight_table, plane.shape[1]),
        plane,
        precision=lax.Precision.HIGHEST,
        preferred_element_type=jnp.float32,
    )


def fetch_recycle(plane):
    count = lax.axis_size("gx")
    return passed_along(plane, "gx", 1 - count)


def shards(
    velocity, accumulated, wall_first, wall_second, recycle_rows, weight_index, weight_table
):
    span = velocity.shape[3]
    rows_here = velocity.shape[2]
    lines = velocity.reshape(-1, span)
    derived = jnp.dot(
        lines,
        spanwise_table(span),
        precision=lax.Precision.HIGHEST,
        preferred_element_type=jnp.float32,
    )
    span_first = derived[:, :span].reshape(velocity.shape)
    span_second = derived[:, span:].reshape(velocity.shape)
    tendency = -(velocity[2:3] * span_first) + viscosity * span_second
    arrived = fetch_recycle(velocity[:, 0])
    whole_plane = lax.all_gather(arrived, "ga", axis=1, tiled=True)
    start = lax.axis_index("ga") * rows_here
    rows = lax.dynamic_slice_in_dim(recycle_rows, start, rows_here)
    picks = lax.dynamic_slice_in_dim(weight_index, start, rows_here)
    inflow = rescale(whole_plane, rows, picks, weight_table)
    tendency = tendency + streamwise(velocity, inflow)
    tendency = tendency + lax.all_to_all(
        wall_terms(
            lax.all_to_all(velocity, "ga", split_axis=3, concat_axis=2, tiled=True),
            wall_first,
            wall_second,
        ),
        "ga",
        split_axis=2,
        concat_axis=3,
        tiled=True,
    )
    accumulated_next = keep_rate * accumulated + step_size * tendency
    return (velocity + update_rate * accumulated_next, accumulated_next)


MESH = pl.DeviceIdType.MESH
PARTS = 2
TILE = 256
SHIFTS = 2


def folded_tables(length):
    half = length // 2
    apart = np.arange(length)[None, :] - np.arange(length)[:, None]
    apart = np.remainder(apart + half, length) - half
    parity = 1.0 - 2.0 * np.remainder(apart, 2)
    spacing = 2.0 * math.pi / length
    angle = apart * (0.5 * spacing)
    same = apart == 0
    sine = np.where(same, 1.0, np.sin(angle))
    first = np.where(same, 0.0, 0.5 * spacing * parity * np.cos(angle) / sine)
    first = np.where(np.abs(apart) == half, 0.0, first)
    second = np.where(
        same,
        -math.pi * math.pi / 3.0 - spacing * spacing / 6.0,
        -0.5 * spacing * spacing * parity / (sine * sine),
    )
    near = np.concatenate([first[:half, :half], second[:half, :half]], 1)
    far = np.concatenate([first[half:, :half], second[half:, :half]], 1)
    return (
        (0.5 * (near + far)).astype(np.float32),
        (0.5 * (near - far)).astype(np.float32),
    )


def exact_dot(left, right):
    return jnp.dot(
        left, right, precision=lax.Precision.HIGHEST, preferred_element_type=jnp.float32
    )


def section_kernel(
    slabs,
    group,
    vel_hbm,
    first_hbm,
    second_hbm,
    even_hbm,
    odd_hbm,
    entries,
    picks,
    table,
    tend,
    vel,
    wall,
    even,
    odd,
    mix,
    gath,
    ret_src,
    ret_in,
    lo,
    hi,
    inf_src,
    fwd_send,
    fwd_recv,
    ret_send,
    ret_recv,
    lo_send,
    lo_recv,
    hi_send,
    hi_recv,
    inf_send,
    inf_recv,
    load_sem,
):
    gx = lax.axis_index("gx")
    me = lax.axis_index("ga")
    planes, rows, span = vel.shape[1:]
    width = span // PARTS
    half = span // 2
    height = group * rows
    chunks = 3 * PARTS
    not_first = gx > 0
    not_last = gx < slabs - 1
    last = gx == slabs - 1
    source = jnp.logical_and(last, jnp.logical_and(me >= 1, me <= SHIFTS))
    loads = [pltpu.make_async_copy(vel_hbm.at[c], vel.at[c], load_sem.at[c]) for c in range(3)]
    loads += [
        pltpu.make_async_copy(even_hbm, even, load_sem.at[3]),
        pltpu.make_async_copy(odd_hbm, odd, load_sem.at[4]),
        pltpu.make_async_copy(first_hbm, wall.at[pl.ds(0, height)], load_sem.at[5]),
        pltpu.make_async_copy(second_hbm, wall.at[pl.ds(height, height)], load_sem.at[6]),
    ]
    for load in loads:
        load.start()

    def place(t):
        turn = t // PARTS
        c = lax.rem(1 + 2 * turn, 3)
        lanes = pl.ds(pl.multiple_of((t - turn * PARTS) * width, width), width)
        return c, lanes

    def shift(t):
        return 1 + lax.rem(t - (t // PARTS) * PARTS, SHIFTS)

    def plane_of(device, t):
        return lax.rem(device - shift(t) + group, group)

    def fwd(t, d):
        c, lanes = place(t)
        peer = lax.rem(me + d, group)
        return pltpu.make_async_remote_copy(
            src_ref=vel_hbm.at[c, plane_of(peer, t), :, lanes],
            dst_ref=gath.at[c, me, :, lanes],
            send_sem=fwd_send.at[t, d - 1],
            recv_sem=fwd_recv.at[t, d - 1],
            device_id={"ga": peer},
            device_id_type=MESH,
        )

    def ret(t, d):
        c, lanes = place(t)
        peer = lax.rem(me + d, group)
        return pltpu.make_async_remote_copy(
            src_ref=ret_src.at[c, peer, :, lanes],
            dst_ref=ret_in.at[c, plane_of(me, t), :, lanes],
            send_sem=ret_send.at[t, d - 1],
            recv_sem=ret_recv.at[t, d - 1],
            device_id={"ga": peer},
            device_id_type=MESH,
        )

    def inf(t, k):
        c, lanes = place(t)
        return pltpu.make_async_remote_copy(
            src_ref=inf_src.at[c, k, :, lanes],
            dst_ref=lo.at[c, 0, :, lanes],
            send_sem=inf_send.at[t, k],
            recv_sem=inf_recv.at[t],
            device_id={"gx": 0, "ga": k},
            device_id_type=MESH,
        )

    def upward(c):
        return pltpu.make_async_remote_copy(
            src_ref=vel_hbm.at[c],
            dst_ref=lo.at[c],
            send_sem=lo_send.at[c],
            recv_sem=lo_recv.at[c],
            device_id={"gx": lax.rem(gx + 1, slabs)},
            device_id_type=MESH,
        )

    def downward(c):
        return pltpu.make_async_remote_copy(
            src_ref=vel_hbm.at[c],
            dst_ref=hi.at[c],
            send_sem=hi_send.at[c],
            recv_sem=hi_recv.at[c],
            device_id={"gx": lax.rem(gx + slabs - 1, slabs)},
            device_id_type=MESH,
        )

    barrier = pltpu.get_barrier_semaphore()
    for d in range(1, group):
        pl.semaphore_signal(
            barrier, inc=1, device_id={"ga": lax.rem(me + d, group)}, device_id_type=MESH
        )

    @pl.when(not_first)
    def _():
        pl.semaphore_signal(barrier, inc=1, device_id={"gx": gx - 1}, device_id_type=MESH)

    @pl.when(not_last)
    def _():
        pl.semaphore_signal(barrier, inc=1, device_id={"gx": gx + 1}, device_id_type=MESH)

    @pl.when(gx == 0)
    def _():
        for k in range(1, SHIFTS + 1):
            pl.semaphore_signal(
                barrier, inc=1, device_id={"gx": slabs - 1, "ga": k}, device_id_type=MESH
            )

    @pl.when(source)
    def _():
        for k in range(group):
            pl.semaphore_signal(
                barrier, inc=1, device_id={"gx": 0, "ga": k}, device_id_type=MESH
            )

    expected = (
        group
        - 1
        + not_first.astype(jnp.int32)
        + not_last.astype(jnp.int32)
        + SHIFTS * (gx == 0).astype(jnp.int32)
        + group * source.astype(jnp.int32)
    )
    pl.semaphore_wait(barrier, expected)

    def send_fwd(t, carry):
        for d in range(1, group):
            fwd(t, d).start()
        return carry

    lax.fori_loop(0, PARTS, send_fwd, 0)
    for c in range(3):

        @pl.when(not_last)
        def _():
            upward(c).start()

        @pl.when(not_first)
        def _():
            downward(c).start()

    lax.fori_loop(PARTS, chunks, send_fwd, 0)

    for load in loads:
        load.wait()

    @pl.when(source)
    def _():
        levels = lax.broadcasted_iota(jnp.int32, (table.shape[1], height), 0)
        chosen = jnp.where(levels == picks[...], 1.0, 0.0)
        frac = exact_dot(jnp.broadcast_to(table[...], (8, table.shape[1])), chosen)[:1]
        apart = lax.broadcasted_iota(jnp.int32, (height, height), 0) - entries[...]
        upright = jnp.where(apart == 0, 1.0 - frac, jnp.where(apart == 1, frac, 0.0))
        mix[...] = upright.T

    @pl.when(jnp.logical_not(not_last))
    def _():
        for c in range(3):
            hi[c, 0] = vel[c, planes - 1]

    def spanwise_step(c, carry):
        left = vel[c, :, :, :half].reshape(planes * rows, half)
        right = vel[c, :, :, half:].reshape(planes * rows, half)
        sums = exact_dot(left + right, even[...])
        differences = exact_dot(left - right, odd[...])
        for side in range(2):
            both = sums + differences if side == 0 else sums - differences
            lanes = slice(side * half, (side + 1) * half)
            first = both[:, :half].reshape(planes, rows, half)
            second = both[:, half:].reshape(planes, rows, half)
            tend[c, :, :, lanes] = viscosity * second - vel[2, :, :, lanes] * first
        return carry

    lax.fori_loop(0, 3, spanwise_step, 0)

    def wall_step(t, carry):
        c, lanes = place(t)
        for d in range(1, group):
            fwd(t, d).wait_recv()
        gath[c, me, :, lanes] = vel[c, plane_of(me, t), :, lanes]
        columns = gath[c, :, :, lanes].reshape(height, width)
        normal = gath[1, :, :, lanes].reshape(height, width)
        both = exact_dot(wall[...], columns)
        term = viscosity * both[height:] - normal * both[:height]
        ret_src[c, :, :, lanes] = term.reshape(group, rows, width)
        for d in range(1, group):
            ret(t, d).start()
        ret_in[c, plane_of(me, t), :, lanes] = ret_src[c, me, :, lanes]

        @pl.when(jnp.logical_and(last, me == shift(t)))
        def _():
            mixed = exact_dot(mix[...], columns)
            inf_src[c, :, :, lanes] = mixed.reshape(group, rows, width)
            for k in range(group):
                inf(t, k).start()

        return carry

    lax.fori_loop(0, chunks, wall_step, 0)

    def stream_step(turn, carry):
        c = lax.rem(1 + 2 * turn, 3)

        @pl.when(not_first)
        def _():
            upward(c).wait_recv()

        @pl.when(gx == 0)
        def _():
            for part in range(PARTS):
                inf(turn * PARTS + part, 0).wait_recv()

        @pl.when(not_last)
        def _():
            downward(c).wait_recv()

        def tile(i, inner):
            block = i // (span // TILE)
            where = pl.ds(pl.multiple_of(block * 8, 8), 8)
            lanes = pl.ds(pl.multiple_of((i - block * (span // TILE)) * TILE, TILE), TILE)
            line = [
                lo[c, p * not_first.astype(jnp.int32), where, lanes] for p in range(HALO)
            ]
            line += [vel[c, p, where, lanes] for p in range(planes)]
            line += [hi[c, p * not_last.astype(jnp.int32), where, lanes] for p in range(HALO)]
            for x in range(planes):
                middle = x + HALO
                first = None
                second = center_coef * line[middle]
                for m in range(1, HALO + 1):
                    ahead, behind = line[middle + m], line[middle - m]
                    step = first_coef[m - 1] * (ahead - behind)
                    first = step if first is None else first + step
                    second = second + second_coef[m - 1] * (ahead + behind)
                total = viscosity * second - vel[0, x, where, lanes] * first
                tend[c, x, where, lanes] = tend[c, x, where, lanes] + total
            return inner

        lax.fori_loop(0, rows // 8 * (span // TILE), tile, 0)
        return carry

    lax.fori_loop(0, 3, stream_step, 0)

    def last_step(t, carry):
        c, lanes = place(t)
        for d in range(1, group):
            ret(t, d).wait_recv()
        tend[c, :, :, lanes] = tend[c, :, :, lanes] + ret_in[c, :, :, lanes]
        return carry

    lax.fori_loop(0, chunks, last_step, 0)

    def drain(t, carry):
        for d in range(1, group):
            fwd(t, d).wait_send()
            ret(t, d).wait_send()

        @pl.when(jnp.logical_and(last, me == shift(t)))
        def _():
            for k in range(group):
                inf(t, k).wait_send()

        return carry

    lax.fori_loop(0, chunks, drain, 0)
    for c in range(3):

        @pl.when(not_last)
        def _():
            upward(c).wait_send()

        @pl.when(not_first)
        def _():
            downward(c).wait_send()


def fast_shards(
    slabs,
    group,
    velocity,
    accumulated,
    wall_first,
    wall_second,
    recycle_rows,
    weight_index,
    weight_table,
):
    _, planes, rows, span = velocity.shape
    height = rows * group
    chunks = 3 * PARTS
    even, odd = folded_tables(span)
    whole = pl.BlockSpec(memory_space=pltpu.VMEM)
    shape = jax.ShapeDtypeStruct(velocity.shape, jnp.float32)
    dma = pltpu.SemaphoreType.DMA
    slab = pltpu.VMEM((3, planes, rows, span), jnp.float32)
    exchanged = pltpu.VMEM((3, group, rows, span), jnp.float32)
    halo = pltpu.VMEM((3, HALO, rows, span), jnp.float32)
    tendency = pl.pallas_call(
        functools.partial(section_kernel, slabs, group),
        out_shape=shape,
        in_specs=[pl.BlockSpec(memory_space=pl.ANY)] * 5 + [whole] * 3,
        out_specs=whole,
        scratch_shapes=[
            slab,
            pltpu.VMEM((2 * height, height), jnp.float32),
            pltpu.VMEM(even.shape, jnp.float32),
            pltpu.VMEM(odd.shape, jnp.float32),
            pltpu.VMEM((height, height), jnp.float32),
            exchanged,
            exchanged,
            slab,
            halo,
            halo,
            exchanged,
            dma((chunks, group - 1)),
            dma((chunks, group - 1)),
            dma((chunks, group - 1)),
            dma((chunks, group - 1)),
            dma((3,)),
            dma((3,)),
            dma((3,)),
            dma((3,)),
            dma((chunks, group)),
            dma((chunks,)),
            dma((7,)),
        ],
        compiler_params=pltpu.CompilerParams(
            collective_id=0, has_side_effects=True, vmem_limit_bytes=60 * 1024 * 1024
        ),
    )(
        velocity,
        wall_first,
        wall_second,
        jnp.asarray(even),
        jnp.asarray(odd),
        recycle_rows.reshape(1, -1),
        weight_index.reshape(1, -1),
        weight_table.reshape(1, -1),
    )
    accumulated_next = keep_rate * accumulated + step_size * tendency
    return (velocity + update_rate * accumulated_next, accumulated_next)


def solution(mesh):
    in_specs = (P(None, "gx", "ga", None), P(None, "gx", "ga", None), P(), P(), P(), P(), P())
    out_specs = (P(None, "gx", "ga", None), P(None, "gx", "ga", None))
    slabs, group = mesh.shape["gx"], mesh.shape["ga"]

    def body(velocity, *others):
        _, planes, rows, span = velocity.shape
        if planes == HALO == group and slabs > 2 and rows % 8 == 0 and span % 768 == 0:
            return fast_shards(slabs, group, velocity, *others)
        return shards(velocity, *others)

    return jax.shard_map(body, mesh=mesh, in_specs=in_specs, out_specs=out_specs, check_vma=False)
```

```python
import functools
import math

import jax
import jax.numpy as jnp
import numpy as np
from jax import lax
from jax.experimental import pallas as pl
from jax.experimental.pallas import tpu as pltpu
from jax.sharding import PartitionSpec as P

HALO = 4


first_coef = (0.8, -0.2, 4.0 / 105.0, -1.0 / 280.0)
second_coef = (1.6, -0.2, 8.0 / 315.0, -1.0 / 560.0)
center_coef = -205.0 / 72.0
step_size = 0.2
viscosity = 0.2
keep_rate = -5.0 / 9.0
update_rate = 15.0 / 16.0


def padded_2(cells, sides, width):
    for axis, dim in sides:
        count = lax.axis_size(axis)
        ends = count - 1
        head = lax.slice_in_dim(cells, 0, width, axis=dim)
        tail = lax.slice_in_dim(cells, cells.shape[dim] - width, cells.shape[dim], axis=dim)
        cells = jnp.concatenate(
            [
                lax.ppermute(tail, axis, [(i, (i + 1) % count) for i in range(ends)]),
                cells,
                lax.ppermute(head, axis, [((i + 1) % count, i) for i in range(ends)]),
            ],
            axis=dim,
        )
    return cells


def passed_along(shard, axis, by):
    peers = lax.axis_size(axis)
    pairs = [(i, i + by) for i in range(peers) if 0 <= i + by < peers]
    return lax.ppermute(shard, axis, pairs)


def spanwise_table(length):
    places = jnp.arange(length, dtype=jnp.int32)
    apart = places[None, :] - places[:, None]
    apart = jnp.remainder(apart + length // 2, length) - length // 2
    parity = 1.0 - 2.0 * jnp.remainder(apart, 2).astype(jnp.float32)
    spacing = 2.0 * math.pi / length
    angle = apart.astype(jnp.float32) * (0.5 * spacing)
    same = apart == 0
    safe_sine = jnp.where(same, 1.0, jnp.sin(angle))
    first = jnp.where(same, 0.0, 0.5 * spacing * parity * jnp.cos(angle) / safe_sine)
    second = jnp.where(
        same,
        -math.pi * math.pi / 3.0 - spacing * spacing / 6.0,
        -0.5 * spacing * spacing * parity / (safe_sine * safe_sine),
    )
    return jnp.concatenate([first, second], 1)


def streamwise(field, inflow):
    extent = field.shape[1]
    padded = padded_2(field, (("gx", 1),), HALO)
    at_inlet = lax.axis_index("gx") == 0
    at_outlet = lax.axis_index("gx") == lax.axis_size("gx") - 1
    ghost_shape = (field.shape[0], HALO) + field.shape[2:]
    lower = jnp.where(at_inlet, jnp.broadcast_to(inflow[:, None], ghost_shape), padded[:, :HALO])
    upper = jnp.where(
        at_outlet, jnp.broadcast_to(field[:, -1:], ghost_shape), padded[:, HALO + extent :]
    )
    padded = jnp.concatenate([lower, field, upper], 1)
    first = jnp.zeros_like(field)
    second = center_coef * field
    for offset in range(1, HALO + 1):
        ahead = padded[:, HALO + offset : HALO + offset + extent]
        behind = padded[:, HALO - offset : HALO - offset + extent]
        first = first + first_coef[offset - 1] * (ahead - behind)
        second = second + second_coef[offset - 1] * (ahead + behind)
    return -(field[0:1] * first) + viscosity * second


def wall_terms(columns, wall_first, wall_second):
    first = jnp.einsum(
        "ij,cxjz->cxiz",
        wall_first,
        columns,
        precision=lax.Precision.HIGHEST,
        preferred_element_type=jnp.float32,
    )
    second = jnp.einsum(
        "ij,cxjz->cxiz",
        wall_second,
        columns,
        precision=lax.Precision.HIGHEST,
        preferred_element_type=jnp.float32,
    )
    return -(columns[1:2] * first) + viscosity * second


def interpolation(rows, picks, weight_table, height):
    levels = jnp.arange(weight_table.shape[0], dtype=jnp.int32)
    frac = jnp.sum(
        jnp.where(picks[:, None] == levels[None, :], weight_table[None, :], 0.0), axis=1
    )[:, None]
    apart = jnp.arange(height, dtype=jnp.int32)[None, :] - rows[:, None]
    return jnp.where(apart == 0, 1.0 - frac, jnp.where(apart == 1, frac, 0.0))


def rescale(plane, rows, picks, weight_table):
    return jnp.einsum(
        "ij,cjz->ciz",
        interpolation(rows, picks, weight_table, plane.shape[1]),
        plane,
        precision=lax.Precision.HIGHEST,
        preferred_element_type=jnp.float32,
    )


def fetch_recycle(plane):
    count = lax.axis_size("gx")
    return passed_along(plane, "gx", 1 - count)


def shards(
    velocity, accumulated, wall_first, wall_second, recycle_rows, weight_index, weight_table
):
    span = velocity.shape[3]
    rows_here = velocity.shape[2]
    lines = velocity.reshape(-1, span)
    derived = jnp.dot(
        lines,
        spanwise_table(span),
        precision=lax.Precision.HIGHEST,
        preferred_element_type=jnp.float32,
    )
    span_first = derived[:, :span].reshape(velocity.shape)
    span_second = derived[:, span:].reshape(velocity.shape)
    tendency = -(velocity[2:3] * span_first) + viscosity * span_second
    arrived = fetch_recycle(velocity[:, 0])
    whole_plane = lax.all_gather(arrived, "ga", axis=1, tiled=True)
    start = lax.axis_index("ga") * rows_here
    rows = lax.dynamic_slice_in_dim(recycle_rows, start, rows_here)
    picks = lax.dynamic_slice_in_dim(weight_index, start, rows_here)
    inflow = rescale(whole_plane, rows, picks, weight_table)
    tendency = tendency + streamwise(velocity, inflow)
    tendency = tendency + lax.all_to_all(
        wall_terms(
            lax.all_to_all(velocity, "ga", split_axis=3, concat_axis=2, tiled=True),
            wall_first,
            wall_second,
        ),
        "ga",
        split_axis=2,
        concat_axis=3,
        tiled=True,
    )
    accumulated_next = keep_rate * accumulated + step_size * tendency
    return (velocity + update_rate * accumulated_next, accumulated_next)


MESH = pl.DeviceIdType.MESH
PARTS = 2
TILE = 256
SHIFTS = 2


def folded_tables(length):
    half = length // 2
    apart = np.arange(length)[None, :] - np.arange(length)[:, None]
    apart = np.remainder(apart + half, length) - half
    parity = 1.0 - 2.0 * np.remainder(apart, 2)
    spacing = 2.0 * math.pi / length
    angle = apart * (0.5 * spacing)
    same = apart == 0
    sine = np.where(same, 1.0, np.sin(angle))
    first = np.where(same, 0.0, 0.5 * spacing * parity * np.cos(angle) / sine)
    first = np.where(np.abs(apart) == half, 0.0, first)
    second = np.where(
        same,
        -math.pi * math.pi / 3.0 - spacing * spacing / 6.0,
        -0.5 * spacing * spacing * parity / (sine * sine),
    )
    near = np.concatenate([first[:half, :half], second[:half, :half]], 1)
    far = np.concatenate([first[half:, :half], second[half:, :half]], 1)
    return (
        (0.5 * (near + far)).astype(np.float32),
        (0.5 * (near - far)).astype(np.float32),
    )


def exact_dot(left, right):
    return jnp.dot(
        left, right, precision=lax.Precision.HIGHEST, preferred_element_type=jnp.float32
    )


def section_kernel(
    slabs,
    group,
    vel_hbm,
    first_hbm,
    second_hbm,
    even_hbm,
    odd_hbm,
    entries,
    picks,
    table,
    tend,
    vel,
    wall,
    even,
    odd,
    mix,
    gath,
    ret_src,
    ret_in,
    lo,
    hi,
    inf_src,
    fwd_send,
    fwd_recv,
    ret_send,
    ret_recv,
    lo_send,
    lo_recv,
    hi_send,
    hi_recv,
    inf_send,
    inf_recv,
    load_sem,
):
    gx = lax.axis_index("gx")
    me = lax.axis_index("ga")
    planes, rows, span = vel.shape[1:]
    width = span // PARTS
    half = span // 2
    height = group * rows
    chunks = 3 * PARTS
    not_first = gx > 0
    not_last = gx < slabs - 1
    last = gx == slabs - 1
    source = jnp.logical_and(last, jnp.logical_and(me >= 1, me <= SHIFTS))
    loads = [pltpu.make_async_copy(vel_hbm.at[c], vel.at[c], load_sem.at[c]) for c in range(3)]
    loads += [
        pltpu.make_async_copy(even_hbm, even, load_sem.at[3]),
        pltpu.make_async_copy(odd_hbm, odd, load_sem.at[4]),
        pltpu.make_async_copy(first_hbm, wall.at[pl.ds(0, height)], load_sem.at[5]),
        pltpu.make_async_copy(second_hbm, wall.at[pl.ds(height, height)], load_sem.at[6]),
    ]
    for load in loads:
        load.start()

    def place(t):
        turn = t // PARTS
        c = lax.rem(1 + 2 * turn, 3)
        lanes = pl.ds(pl.multiple_of((t - turn * PARTS) * width, width), width)
        return c, lanes

    def shift(t):
        return 1 + lax.rem(t - (t // PARTS) * PARTS, SHIFTS)

    def plane_of(device, t):
        return lax.rem(device - shift(t) + group, group)

    def fwd(t, d):
        c, lanes = place(t)
        peer = lax.rem(me + d, group)
        return pltpu.make_async_remote_copy(
            src_ref=vel_hbm.at[c, plane_of(peer, t), :, lanes],
            dst_ref=gath.at[c, me, :, lanes],
            send_sem=fwd_send.at[t, d - 1],
            recv_sem=fwd_recv.at[t, d - 1],
            device_id={"ga": peer},
            device_id_type=MESH,
        )

    def ret(t, d):
        c, lanes = place(t)
        peer = lax.rem(me + d, group)
        return pltpu.make_async_remote_copy(
            src_ref=ret_src.at[c, peer, :, lanes],
            dst_ref=ret_in.at[c, plane_of(me, t), :, lanes],
            send_sem=ret_send.at[t, d - 1],
            recv_sem=ret_recv.at[t, d - 1],
            device_id={"ga": peer},
            device_id_type=MESH,
        )

    def inf(t, k):
        c, lanes = place(t)
        return pltpu.make_async_remote_copy(
            src_ref=inf_src.at[c, k, :, lanes],
            dst_ref=lo.at[c, 0, :, lanes],
            send_sem=inf_send.at[t, k],
            recv_sem=inf_recv.at[t],
            device_id={"gx": 0, "ga": k},
            device_id_type=MESH,
        )

    def upward(c):
        return pltpu.make_async_remote_copy(
            src_ref=vel_hbm.at[c],
            dst_ref=lo.at[c],
            send_sem=lo_send.at[c],
            recv_sem=lo_recv.at[c],
            device_id={"gx": lax.rem(gx + 1, slabs)},
            device_id_type=MESH,
        )

    def downward(c):
        return pltpu.make_async_remote_copy(
            src_ref=vel_hbm.at[c],
            dst_ref=hi.at[c],
            send_sem=hi_send.at[c],
            recv_sem=hi_recv.at[c],
            device_id={"gx": lax.rem(gx + slabs - 1, slabs)},
            device_id_type=MESH,
        )

    barrier = pltpu.get_barrier_semaphore()
    for d in range(1, group):
        pl.semaphore_signal(
            barrier, inc=1, device_id={"ga": lax.rem(me + d, group)}, device_id_type=MESH
        )

    @pl.when(not_first)
    def _():
        pl.semaphore_signal(barrier, inc=1, device_id={"gx": gx - 1}, device_id_type=MESH)

    @pl.when(not_last)
    def _():
        pl.semaphore_signal(barrier, inc=1, device_id={"gx": gx + 1}, device_id_type=MESH)

    @pl.when(gx == 0)
    def _():
        for k in range(1, SHIFTS + 1):
            pl.semaphore_signal(
                barrier, inc=1, device_id={"gx": slabs - 1, "ga": k}, device_id_type=MESH
            )

    @pl.when(source)
    def _():
        for k in range(group):
            pl.semaphore_signal(
                barrier, inc=1, device_id={"gx": 0, "ga": k}, device_id_type=MESH
            )

    expected = (
        group
        - 1
        + not_first.astype(jnp.int32)
        + not_last.astype(jnp.int32)
        + SHIFTS * (gx == 0).astype(jnp.int32)
        + group * source.astype(jnp.int32)
    )
    pl.semaphore_wait(barrier, expected)

    def mixes(t, device):
        return jnp.logical_and(last, device == shift(t))

    def send_recycle(t, carry):
        for d in range(1, group):

            @pl.when(mixes(t, lax.rem(me + d, group)))
            def _():
                fwd(t, d).start()

        return carry

    lax.fori_loop(0, chunks, send_recycle, 0)

    def send_fwd(t, carry):
        for d in range(1, group):

            @pl.when(jnp.logical_not(mixes(t, lax.rem(me + d, group))))
            def _():
                fwd(t, d).start()

        return carry

    lax.fori_loop(0, PARTS, send_fwd, 0)
    for c in range(3):

        @pl.when(not_last)
        def _():
            upward(c).start()

        @pl.when(not_first)
        def _():
            downward(c).start()

    lax.fori_loop(PARTS, chunks, send_fwd, 0)

    for load in loads:
        load.wait()

    @pl.when(source)
    def _():
        levels = lax.broadcasted_iota(jnp.int32, (table.shape[1], height), 0)
        chosen = jnp.where(levels == picks[...].reshape(1, height), 1.0, 0.0)
        frac = exact_dot(jnp.broadcast_to(table[...], (8, table.shape[1])), chosen)[:1]
        apart = lax.broadcasted_iota(jnp.int32, (height, height), 0)
        apart = apart - entries[...].reshape(1, height)
        upright = jnp.where(apart == 0, 1.0 - frac, jnp.where(apart == 1, frac, 0.0))
        mix[...] = upright.T

    @pl.when(jnp.logical_not(not_last))
    def _():
        for c in range(3):
            hi[c, 0] = vel[c, planes - 1]

    def inflow_step(t, carry):
        @pl.when(mixes(t, me))
        def _():
            c, lanes = place(t)
            for d in range(1, group):
                fwd(t, d).wait_recv()
            gath[c, me, :, lanes] = vel[c, plane_of(me, t), :, lanes]
            columns = gath[c, :, :, lanes].reshape(height, width)
            mixed = exact_dot(mix[...], columns)
            inf_src[c, :, :, lanes] = mixed.reshape(group, rows, width)
            for k in range(group):
                inf(t, k).start()

        return carry

    lax.fori_loop(0, chunks, inflow_step, 0)

    def spanwise_step(c, carry):
        left = vel[c, :, :, :half].reshape(planes * rows, half)
        right = vel[c, :, :, half:].reshape(planes * rows, half)
        sums = exact_dot(left + right, even[...])
        differences = exact_dot(left - right, odd[...])
        for side in range(2):
            both = sums + differences if side == 0 else sums - differences
            lanes = slice(side * half, (side + 1) * half)
            first = both[:, :half].reshape(planes, rows, half)
            second = both[:, half:].reshape(planes, rows, half)
            tend[c, :, :, lanes] = viscosity * second - vel[2, :, :, lanes] * first
        return carry

    lax.fori_loop(0, 3, spanwise_step, 0)

    def wall_step(t, carry):
        c, lanes = place(t)
        @pl.when(jnp.logical_not(mixes(t, me)))
        def _():
            for d in range(1, group):
                fwd(t, d).wait_recv()

        gath[c, me, :, lanes] = vel[c, plane_of(me, t), :, lanes]
        columns = gath[c, :, :, lanes].reshape(height, width)
        normal = gath[1, :, :, lanes].reshape(height, width)
        both = exact_dot(wall[...], columns)
        term = viscosity * both[height:] - normal * both[:height]
        ret_src[c, :, :, lanes] = term.reshape(group, rows, width)
        for d in range(1, group):
            ret(t, d).start()
        ret_in[c, plane_of(me, t), :, lanes] = ret_src[c, me, :, lanes]

        return carry

    lax.fori_loop(0, chunks, wall_step, 0)

    def stream_step(turn, carry):
        c = lax.rem(1 + 2 * turn, 3)

        @pl.when(not_first)
        def _():
            upward(c).wait_recv()

        @pl.when(gx == 0)
        def _():
            for part in range(PARTS):
                inf(turn * PARTS + part, 0).wait_recv()

        @pl.when(not_last)
        def _():
            downward(c).wait_recv()

        def tile(i, inner):
            block = i // (span // TILE)
            where = pl.ds(pl.multiple_of(block * 8, 8), 8)
            lanes = pl.ds(pl.multiple_of((i - block * (span // TILE)) * TILE, TILE), TILE)
            line = [
                lo[c, p * not_first.astype(jnp.int32), where, lanes] for p in range(HALO)
            ]
            line += [vel[c, p, where, lanes] for p in range(planes)]
            line += [hi[c, p * not_last.astype(jnp.int32), where, lanes] for p in range(HALO)]
            for x in range(planes):
                middle = x + HALO
                first = None
                second = center_coef * line[middle]
                for m in range(1, HALO + 1):
                    ahead, behind = line[middle + m], line[middle - m]
                    step = first_coef[m - 1] * (ahead - behind)
                    first = step if first is None else first + step
                    second = second + second_coef[m - 1] * (ahead + behind)
                total = viscosity * second - vel[0, x, where, lanes] * first
                tend[c, x, where, lanes] = tend[c, x, where, lanes] + total
            return inner

        lax.fori_loop(0, rows // 8 * (span // TILE), tile, 0)
        return carry

    lax.fori_loop(0, 3, stream_step, 0)

    def last_step(t, carry):
        c, lanes = place(t)
        for d in range(1, group):
            ret(t, d).wait_recv()
        tend[c, :, :, lanes] = tend[c, :, :, lanes] + ret_in[c, :, :, lanes]
        return carry

    lax.fori_loop(0, chunks, last_step, 0)

    def drain(t, carry):
        for d in range(1, group):
            fwd(t, d).wait_send()
            ret(t, d).wait_send()

        @pl.when(jnp.logical_and(last, me == shift(t)))
        def _():
            for k in range(group):
                inf(t, k).wait_send()

        return carry

    lax.fori_loop(0, chunks, drain, 0)
    for c in range(3):

        @pl.when(not_last)
        def _():
            upward(c).wait_send()

        @pl.when(not_first)
        def _():
            downward(c).wait_send()


def fast_shards(
    slabs,
    group,
    velocity,
    accumulated,
    wall_first,
    wall_second,
    recycle_rows,
    weight_index,
    weight_table,
):
    _, planes, rows, span = velocity.shape
    height = rows * group
    chunks = 3 * PARTS
    even, odd = folded_tables(span)
    whole = pl.BlockSpec(memory_space=pltpu.VMEM)
    shape = jax.ShapeDtypeStruct(velocity.shape, jnp.float32)
    dma = pltpu.SemaphoreType.DMA
    slab = pltpu.VMEM((3, planes, rows, span), jnp.float32)
    exchanged = pltpu.VMEM((3, group, rows, span), jnp.float32)
    halo = pltpu.VMEM((3, HALO, rows, span), jnp.float32)
    tendency = pl.pallas_call(
        functools.partial(section_kernel, slabs, group),
        out_shape=shape,
        in_specs=[pl.BlockSpec(memory_space=pl.ANY)] * 5 + [whole] * 3,
        out_specs=whole,
        scratch_shapes=[
            slab,
            pltpu.VMEM((2 * height, height), jnp.float32),
            pltpu.VMEM(even.shape, jnp.float32),
            pltpu.VMEM(odd.shape, jnp.float32),
            pltpu.VMEM((height, height), jnp.float32),
            exchanged,
            exchanged,
            slab,
            halo,
            halo,
            exchanged,
            dma((chunks, group - 1)),
            dma((chunks, group - 1)),
            dma((chunks, group - 1)),
            dma((chunks, group - 1)),
            dma((3,)),
            dma((3,)),
            dma((3,)),
            dma((3,)),
            dma((chunks, group)),
            dma((chunks,)),
            dma((7,)),
        ],
        compiler_params=pltpu.CompilerParams(
            collective_id=0, has_side_effects=True, vmem_limit_bytes=60 * 1024 * 1024
        ),
    )(
        velocity,
        wall_first,
        wall_second,
        jnp.asarray(even),
        jnp.asarray(odd),
        recycle_rows,
        weight_index,
        weight_table.reshape(1, -1),
    )
    accumulated_next = keep_rate * accumulated + step_size * tendency
    return (velocity + update_rate * accumulated_next, accumulated_next)


def solution(mesh):
    in_specs = (P(None, "gx", "ga", None), P(None, "gx", "ga", None), P(), P(), P(), P(), P())
    out_specs = (P(None, "gx", "ga", None), P(None, "gx", "ga", None))
    slabs, group = mesh.shape["gx"], mesh.shape["ga"]

    def body(velocity, *others):
        _, planes, rows, span = velocity.shape
        if planes == HALO == group and slabs > 2 and rows % 8 == 0 and span % 768 == 0:
            return fast_shards(slabs, group, velocity, *others)
        return shards(velocity, *others)

    return jax.shard_map(body, mesh=mesh, in_specs=in_specs, out_specs=out_specs, check_vma=False)
```

```python
import functools
import math

import jax
import jax.numpy as jnp
import numpy as np
from jax import lax
from jax.experimental import pallas as pl
from jax.experimental.pallas import tpu as pltpu
from jax.sharding import PartitionSpec as P

HALO = 4


first_coef = (0.8, -0.2, 4.0 / 105.0, -1.0 / 280.0)
second_coef = (1.6, -0.2, 8.0 / 315.0, -1.0 / 560.0)
center_coef = -205.0 / 72.0
step_size = 0.2
viscosity = 0.2
keep_rate = -5.0 / 9.0
update_rate = 15.0 / 16.0


def padded_2(cells, sides, width):
    for axis, dim in sides:
        count = lax.axis_size(axis)
        ends = count - 1
        head = lax.slice_in_dim(cells, 0, width, axis=dim)
        tail = lax.slice_in_dim(cells, cells.shape[dim] - width, cells.shape[dim], axis=dim)
        cells = jnp.concatenate(
            [
                lax.ppermute(tail, axis, [(i, (i + 1) % count) for i in range(ends)]),
                cells,
                lax.ppermute(head, axis, [((i + 1) % count, i) for i in range(ends)]),
            ],
            axis=dim,
        )
    return cells


def passed_along(shard, axis, by):
    peers = lax.axis_size(axis)
    pairs = [(i, i + by) for i in range(peers) if 0 <= i + by < peers]
    return lax.ppermute(shard, axis, pairs)


def spanwise_table(length):
    places = jnp.arange(length, dtype=jnp.int32)
    apart = places[None, :] - places[:, None]
    apart = jnp.remainder(apart + length // 2, length) - length // 2
    parity = 1.0 - 2.0 * jnp.remainder(apart, 2).astype(jnp.float32)
    spacing = 2.0 * math.pi / length
    angle = apart.astype(jnp.float32) * (0.5 * spacing)
    same = apart == 0
    safe_sine = jnp.where(same, 1.0, jnp.sin(angle))
    first = jnp.where(same, 0.0, 0.5 * spacing * parity * jnp.cos(angle) / safe_sine)
    second = jnp.where(
        same,
        -math.pi * math.pi / 3.0 - spacing * spacing / 6.0,
        -0.5 * spacing * spacing * parity / (safe_sine * safe_sine),
    )
    return jnp.concatenate([first, second], 1)


def streamwise(field, inflow):
    extent = field.shape[1]
    padded = padded_2(field, (("gx", 1),), HALO)
    at_inlet = lax.axis_index("gx") == 0
    at_outlet = lax.axis_index("gx") == lax.axis_size("gx") - 1
    ghost_shape = (field.shape[0], HALO) + field.shape[2:]
    lower = jnp.where(at_inlet, jnp.broadcast_to(inflow[:, None], ghost_shape), padded[:, :HALO])
    upper = jnp.where(
        at_outlet, jnp.broadcast_to(field[:, -1:], ghost_shape), padded[:, HALO + extent :]
    )
    padded = jnp.concatenate([lower, field, upper], 1)
    first = jnp.zeros_like(field)
    second = center_coef * field
    for offset in range(1, HALO + 1):
        ahead = padded[:, HALO + offset : HALO + offset + extent]
        behind = padded[:, HALO - offset : HALO - offset + extent]
        first = first + first_coef[offset - 1] * (ahead - behind)
        second = second + second_coef[offset - 1] * (ahead + behind)
    return -(field[0:1] * first) + viscosity * second


def wall_terms(columns, wall_first, wall_second):
    first = jnp.einsum(
        "ij,cxjz->cxiz",
        wall_first,
        columns,
        precision=lax.Precision.HIGHEST,
        preferred_element_type=jnp.float32,
    )
    second = jnp.einsum(
        "ij,cxjz->cxiz",
        wall_second,
        columns,
        precision=lax.Precision.HIGHEST,
        preferred_element_type=jnp.float32,
    )
    return -(columns[1:2] * first) + viscosity * second


def interpolation(rows, picks, weight_table, height):
    levels = jnp.arange(weight_table.shape[0], dtype=jnp.int32)
    frac = jnp.sum(
        jnp.where(picks[:, None] == levels[None, :], weight_table[None, :], 0.0), axis=1
    )[:, None]
    apart = jnp.arange(height, dtype=jnp.int32)[None, :] - rows[:, None]
    return jnp.where(apart == 0, 1.0 - frac, jnp.where(apart == 1, frac, 0.0))


def rescale(plane, rows, picks, weight_table):
    return jnp.einsum(
        "ij,cjz->ciz",
        interpolation(rows, picks, weight_table, plane.shape[1]),
        plane,
        precision=lax.Precision.HIGHEST,
        preferred_element_type=jnp.float32,
    )


def fetch_recycle(plane):
    count = lax.axis_size("gx")
    return passed_along(plane, "gx", 1 - count)


def shards(
    velocity, accumulated, wall_first, wall_second, recycle_rows, weight_index, weight_table
):
    span = velocity.shape[3]
    rows_here = velocity.shape[2]
    lines = velocity.reshape(-1, span)
    derived = jnp.dot(
        lines,
        spanwise_table(span),
        precision=lax.Precision.HIGHEST,
        preferred_element_type=jnp.float32,
    )
    span_first = derived[:, :span].reshape(velocity.shape)
    span_second = derived[:, span:].reshape(velocity.shape)
    tendency = -(velocity[2:3] * span_first) + viscosity * span_second
    arrived = fetch_recycle(velocity[:, 0])
    whole_plane = lax.all_gather(arrived, "ga", axis=1, tiled=True)
    start = lax.axis_index("ga") * rows_here
    rows = lax.dynamic_slice_in_dim(recycle_rows, start, rows_here)
    picks = lax.dynamic_slice_in_dim(weight_index, start, rows_here)
    inflow = rescale(whole_plane, rows, picks, weight_table)
    tendency = tendency + streamwise(velocity, inflow)
    tendency = tendency + lax.all_to_all(
        wall_terms(
            lax.all_to_all(velocity, "ga", split_axis=3, concat_axis=2, tiled=True),
            wall_first,
            wall_second,
        ),
        "ga",
        split_axis=2,
        concat_axis=3,
        tiled=True,
    )
    accumulated_next = keep_rate * accumulated + step_size * tendency
    return (velocity + update_rate * accumulated_next, accumulated_next)


MESH = pl.DeviceIdType.MESH
PARTS = 2
TILE = 256
SHIFTS = 2


def folded_tables(length):
    half = length // 2
    apart = np.arange(length)[None, :] - np.arange(length)[:, None]
    apart = np.remainder(apart + half, length) - half
    parity = 1.0 - 2.0 * np.remainder(apart, 2)
    spacing = 2.0 * math.pi / length
    angle = apart * (0.5 * spacing)
    same = apart == 0
    sine = np.where(same, 1.0, np.sin(angle))
    first = np.where(same, 0.0, 0.5 * spacing * parity * np.cos(angle) / sine)
    first = np.where(np.abs(apart) == half, 0.0, first)
    second = np.where(
        same,
        -math.pi * math.pi / 3.0 - spacing * spacing / 6.0,
        -0.5 * spacing * spacing * parity / (sine * sine),
    )
    near = np.concatenate([first[:half, :half], second[:half, :half]], 1)
    far = np.concatenate([first[half:, :half], second[half:, :half]], 1)
    return (
        (0.5 * (near + far)).astype(np.float32),
        (0.5 * (near - far)).astype(np.float32),
    )


def exact_dot(left, right):
    return jnp.dot(
        left, right, precision=lax.Precision.HIGHEST, preferred_element_type=jnp.float32
    )


def section_kernel(
    slabs,
    group,
    vel_hbm,
    first_hbm,
    second_hbm,
    even_hbm,
    odd_hbm,
    entries,
    picks,
    table,
    tend,
    vel,
    wall,
    even,
    odd,
    mix,
    gath,
    ret_src,
    ret_in,
    lo,
    hi,
    inf_src,
    fwd_send,
    fwd_recv,
    ret_send,
    ret_recv,
    lo_send,
    lo_recv,
    hi_send,
    hi_recv,
    inf_send,
    inf_recv,
    load_sem,
    relay,
    relay_send,
    relay_recv,
):
    gx = lax.axis_index("gx")
    me = lax.axis_index("ga")
    planes, rows, span = vel.shape[1:]
    width = span // PARTS
    half = span // 2
    height = group * rows
    chunks = 3 * PARTS
    not_first = gx > 0
    not_last = gx < slabs - 1
    last = gx == slabs - 1
    source = jnp.logical_and(last, jnp.logical_and(me >= 1, me <= SHIFTS))
    inner = jnp.logical_and(me >= 1, me <= SHIFTS)
    middle_relay = jnp.logical_and(gx == 2, inner)
    inlet_relay = jnp.logical_and(gx == 0, inner)
    loads = [pltpu.make_async_copy(vel_hbm.at[c], vel.at[c], load_sem.at[c]) for c in range(3)]
    loads += [
        pltpu.make_async_copy(even_hbm, even, load_sem.at[3]),
        pltpu.make_async_copy(odd_hbm, odd, load_sem.at[4]),
        pltpu.make_async_copy(first_hbm, wall.at[pl.ds(0, height)], load_sem.at[5]),
        pltpu.make_async_copy(second_hbm, wall.at[pl.ds(height, height)], load_sem.at[6]),
    ]
    for load in loads:
        load.start()

    def place(t):
        turn = t // PARTS
        c = lax.rem(1 + 2 * turn, 3)
        lanes = pl.ds(pl.multiple_of((t - turn * PARTS) * width, width), width)
        return c, lanes

    def shift(t):
        return 1 + lax.rem(t - (t // PARTS) * PARTS, SHIFTS)

    def plane_of(device, t):
        return lax.rem(device - shift(t) + group, group)

    def fwd(t, d):
        c, lanes = place(t)
        peer = lax.rem(me + d, group)
        return pltpu.make_async_remote_copy(
            src_ref=vel_hbm.at[c, plane_of(peer, t), :, lanes],
            dst_ref=gath.at[c, me, :, lanes],
            send_sem=fwd_send.at[t, d - 1],
            recv_sem=fwd_recv.at[t, d - 1],
            device_id={"ga": peer},
            device_id_type=MESH,
        )

    def ret(t, d):
        c, lanes = place(t)
        peer = lax.rem(me + d, group)
        return pltpu.make_async_remote_copy(
            src_ref=ret_src.at[c, peer, :, lanes],
            dst_ref=ret_in.at[c, plane_of(me, t), :, lanes],
            send_sem=ret_send.at[t, d - 1],
            recv_sem=ret_recv.at[t, d - 1],
            device_id={"ga": peer},
            device_id_type=MESH,
        )

    def inf(t, k):
        c, lanes = place(t)
        return pltpu.make_async_remote_copy(
            src_ref=inf_src.at[c, k, :, lanes],
            dst_ref=lo.at[c, 0, :, lanes],
            send_sem=inf_send.at[t, k],
            recv_sem=inf_recv.at[t],
            device_id={"gx": 0, "ga": k},
            device_id_type=MESH,
        )

    def to_relay(turn):
        t = turn * PARTS + me - 1
        c, lanes = place(t)
        return pltpu.make_async_remote_copy(
            src_ref=inf_src.at[c, :, :, lanes],
            dst_ref=relay,
            send_sem=inf_send.at[t, 0],
            recv_sem=relay_recv.at[0],
            device_id={"gx": 2 * turn},
            device_id_type=MESH,
        )

    def from_relay(turn, k):
        t = turn * PARTS + me - 1
        c, lanes = place(t)
        return pltpu.make_async_remote_copy(
            src_ref=relay.at[k],
            dst_ref=lo.at[c, 0, :, lanes],
            send_sem=relay_send.at[k],
            recv_sem=inf_recv.at[t],
            device_id={"gx": 0, "ga": k},
            device_id_type=MESH,
        )

    def own_relay():
        c, lanes = place(me - 1)
        return pltpu.make_async_copy(
            relay.at[me], lo.at[c, 0, :, lanes], inf_recv.at[me - 1]
        )

    def upward(c):
        return pltpu.make_async_remote_copy(
            src_ref=vel_hbm.at[c],
            dst_ref=lo.at[c],
            send_sem=lo_send.at[c],
            recv_sem=lo_recv.at[c],
            device_id={"gx": lax.rem(gx + 1, slabs)},
            device_id_type=MESH,
        )

    def downward(c):
        return pltpu.make_async_remote_copy(
            src_ref=vel_hbm.at[c],
            dst_ref=hi.at[c],
            send_sem=hi_send.at[c],
            recv_sem=hi_recv.at[c],
            device_id={"gx": lax.rem(gx + slabs - 1, slabs)},
            device_id_type=MESH,
        )

    barrier = pltpu.get_barrier_semaphore()
    for d in range(1, group):
        pl.semaphore_signal(
            barrier, inc=1, device_id={"ga": lax.rem(me + d, group)}, device_id_type=MESH
        )

    @pl.when(not_first)
    def _():
        pl.semaphore_signal(barrier, inc=1, device_id={"gx": gx - 1}, device_id_type=MESH)

    @pl.when(not_last)
    def _():
        pl.semaphore_signal(barrier, inc=1, device_id={"gx": gx + 1}, device_id_type=MESH)

    @pl.when(gx == 0)
    def _():
        for k in range(1, SHIFTS + 1):
            pl.semaphore_signal(
                barrier, inc=1, device_id={"gx": slabs - 1, "ga": k}, device_id_type=MESH
            )

    @pl.when(source)
    def _():
        for k in range(group):
            pl.semaphore_signal(
                barrier, inc=1, device_id={"gx": 0, "ga": k}, device_id_type=MESH
            )

    @pl.when(gx == 0)
    def _():
        for k in range(1, SHIFTS + 1):
            pl.semaphore_signal(
                barrier, inc=1, device_id={"gx": 2, "ga": k}, device_id_type=MESH
            )

    @pl.when(source)
    def _():
        pl.semaphore_signal(barrier, inc=1, device_id={"gx": 2}, device_id_type=MESH)

    @pl.when(middle_relay)
    def _():
        pl.semaphore_signal(barrier, inc=1, device_id={"gx": slabs - 1}, device_id_type=MESH)
        for k in range(group):
            pl.semaphore_signal(
                barrier, inc=1, device_id={"gx": 0, "ga": k}, device_id_type=MESH
            )

    expected = (
        group
        - 1
        + not_first.astype(jnp.int32)
        + not_last.astype(jnp.int32)
        + 2 * SHIFTS * (gx == 0).astype(jnp.int32)
        + (group + 1) * source.astype(jnp.int32)
        + (group + 1) * middle_relay.astype(jnp.int32)
    )
    pl.semaphore_wait(barrier, expected)

    def mixes(t, device):
        return jnp.logical_and(last, device == shift(t))

    def send_recycle(t, carry):
        for d in range(1, group):

            @pl.when(mixes(t, lax.rem(me + d, group)))
            def _():
                fwd(t, d).start()

        return carry

    lax.fori_loop(0, chunks, send_recycle, 0)

    def send_fwd(t, carry):
        for d in range(1, group):

            @pl.when(jnp.logical_not(mixes(t, lax.rem(me + d, group))))
            def _():
                fwd(t, d).start()

        return carry

    lax.fori_loop(0, PARTS, send_fwd, 0)
    for c in range(3):

        @pl.when(not_last)
        def _():
            upward(c).start()

        @pl.when(not_first)
        def _():
            downward(c).start()

    lax.fori_loop(PARTS, chunks, send_fwd, 0)

    for load in loads:
        load.wait()

    @pl.when(source)
    def _():
        levels = lax.broadcasted_iota(jnp.int32, (table.shape[1], height), 0)
        chosen = jnp.where(levels == picks[...].reshape(1, height), 1.0, 0.0)
        frac = exact_dot(jnp.broadcast_to(table[...], (8, table.shape[1])), chosen)[:1]
        apart = lax.broadcasted_iota(jnp.int32, (height, height), 0)
        apart = apart - entries[...].reshape(1, height)
        upright = jnp.where(apart == 0, 1.0 - frac, jnp.where(apart == 1, frac, 0.0))
        mix[...] = upright.T

    @pl.when(jnp.logical_not(not_last))
    def _():
        for c in range(3):
            hi[c, 0] = vel[c, planes - 1]

    def inflow_step(t, carry):
        @pl.when(mixes(t, me))
        def _():
            c, lanes = place(t)
            for d in range(1, group):
                fwd(t, d).wait_recv()
            gath[c, me, :, lanes] = vel[c, plane_of(me, t), :, lanes]
            columns = gath[c, :, :, lanes].reshape(height, width)
            mixed = exact_dot(mix[...], columns)
            inf_src[c, :, :, lanes] = mixed.reshape(group, rows, width)
            for turn in range(2):

                @pl.when(t // PARTS == turn)
                def _():
                    to_relay(turn).start()

            @pl.when(t // PARTS == 2)
            def _():
                for k in range(group):
                    inf(t, k).start()

        return carry

    lax.fori_loop(0, chunks, inflow_step, 0)

    def spanwise_step(c, carry):
        left = vel[c, :, :, :half].reshape(planes * rows, half)
        right = vel[c, :, :, half:].reshape(planes * rows, half)
        sums = exact_dot(left + right, even[...])
        differences = exact_dot(left - right, odd[...])
        for side in range(2):
            both = sums + differences if side == 0 else sums - differences
            lanes = slice(side * half, (side + 1) * half)
            first = both[:, :half].reshape(planes, rows, half)
            second = both[:, half:].reshape(planes, rows, half)
            tend[c, :, :, lanes] = viscosity * second - vel[2, :, :, lanes] * first
        return carry

    lax.fori_loop(0, 3, spanwise_step, 0)

    @pl.when(inlet_relay)
    def _():
        to_relay(0).wait_recv()
        own_relay().start()
        for d in range(1, group):
            from_relay(0, lax.rem(me + d, group)).start()

    @pl.when(middle_relay)
    def _():
        to_relay(1).wait_recv()
        for k in range(group):
            from_relay(1, k).start()

    def wall_step(t, carry):
        c, lanes = place(t)
        @pl.when(jnp.logical_not(mixes(t, me)))
        def _():
            for d in range(1, group):
                fwd(t, d).wait_recv()

        gath[c, me, :, lanes] = vel[c, plane_of(me, t), :, lanes]
        columns = gath[c, :, :, lanes].reshape(height, width)
        normal = gath[1, :, :, lanes].reshape(height, width)
        both = exact_dot(wall[...], columns)
        term = viscosity * both[height:] - normal * both[:height]
        ret_src[c, :, :, lanes] = term.reshape(group, rows, width)
        for d in range(1, group):
            ret(t, d).start()
        ret_in[c, plane_of(me, t), :, lanes] = ret_src[c, me, :, lanes]

        return carry

    lax.fori_loop(0, chunks, wall_step, 0)

    def stream_step(turn, carry):
        c = lax.rem(1 + 2 * turn, 3)

        @pl.when(not_first)
        def _():
            upward(c).wait_recv()

        @pl.when(gx == 0)
        def _():
            for part in range(PARTS):
                inf(turn * PARTS + part, 0).wait_recv()

        @pl.when(not_last)
        def _():
            downward(c).wait_recv()

        def tile(i, inner):
            block = i // (span // TILE)
            where = pl.ds(pl.multiple_of(block * 8, 8), 8)
            lanes = pl.ds(pl.multiple_of((i - block * (span // TILE)) * TILE, TILE), TILE)
            line = [
                lo[c, p * not_first.astype(jnp.int32), where, lanes] for p in range(HALO)
            ]
            line += [vel[c, p, where, lanes] for p in range(planes)]
            line += [hi[c, p * not_last.astype(jnp.int32), where, lanes] for p in range(HALO)]
            for x in range(planes):
                middle = x + HALO
                first = None
                second = center_coef * line[middle]
                for m in range(1, HALO + 1):
                    ahead, behind = line[middle + m], line[middle - m]
                    step = first_coef[m - 1] * (ahead - behind)
                    first = step if first is None else first + step
                    second = second + second_coef[m - 1] * (ahead + behind)
                total = viscosity * second - vel[0, x, where, lanes] * first
                tend[c, x, where, lanes] = tend[c, x, where, lanes] + total
            return inner

        lax.fori_loop(0, rows // 8 * (span // TILE), tile, 0)
        return carry

    lax.fori_loop(0, 3, stream_step, 0)

    def last_step(t, carry):
        c, lanes = place(t)
        for d in range(1, group):
            ret(t, d).wait_recv()
        tend[c, :, :, lanes] = tend[c, :, :, lanes] + ret_in[c, :, :, lanes]
        return carry

    lax.fori_loop(0, chunks, last_step, 0)

    def drain(t, carry):
        for d in range(1, group):
            fwd(t, d).wait_send()
            ret(t, d).wait_send()

        @pl.when(jnp.logical_and(last, me == shift(t)))
        def _():
            for turn in range(2):

                @pl.when(t // PARTS == turn)
                def _():
                    to_relay(turn).wait_send()

            @pl.when(t // PARTS == 2)
            def _():
                for k in range(group):
                    inf(t, k).wait_send()

        return carry

    lax.fori_loop(0, chunks, drain, 0)

    @pl.when(inlet_relay)
    def _():
        for d in range(1, group):
            from_relay(0, lax.rem(me + d, group)).wait_send()

    @pl.when(middle_relay)
    def _():
        for k in range(group):
            from_relay(1, k).wait_send()

    for c in range(3):

        @pl.when(not_last)
        def _():
            upward(c).wait_send()

        @pl.when(not_first)
        def _():
            downward(c).wait_send()


def fast_shards(
    slabs,
    group,
    velocity,
    accumulated,
    wall_first,
    wall_second,
    recycle_rows,
    weight_index,
    weight_table,
):
    _, planes, rows, span = velocity.shape
    height = rows * group
    chunks = 3 * PARTS
    even, odd = folded_tables(span)
    whole = pl.BlockSpec(memory_space=pltpu.VMEM)
    shape = jax.ShapeDtypeStruct(velocity.shape, jnp.float32)
    dma = pltpu.SemaphoreType.DMA
    slab = pltpu.VMEM((3, planes, rows, span), jnp.float32)
    exchanged = pltpu.VMEM((3, group, rows, span), jnp.float32)
    halo = pltpu.VMEM((3, HALO, rows, span), jnp.float32)
    tendency = pl.pallas_call(
        functools.partial(section_kernel, slabs, group),
        out_shape=shape,
        in_specs=[pl.BlockSpec(memory_space=pl.ANY)] * 5 + [whole] * 3,
        out_specs=whole,
        scratch_shapes=[
            slab,
            pltpu.VMEM((2 * height, height), jnp.float32),
            pltpu.VMEM(even.shape, jnp.float32),
            pltpu.VMEM(odd.shape, jnp.float32),
            pltpu.VMEM((height, height), jnp.float32),
            exchanged,
            exchanged,
            slab,
            halo,
            halo,
            exchanged,
            dma((chunks, group - 1)),
            dma((chunks, group - 1)),
            dma((chunks, group - 1)),
            dma((chunks, group - 1)),
            dma((3,)),
            dma((3,)),
            dma((3,)),
            dma((3,)),
            dma((chunks, group)),
            dma((chunks,)),
            dma((7,)),
            pltpu.VMEM((group, rows, span // PARTS), jnp.float32),
            dma((group,)),
            dma((1,)),
        ],
        compiler_params=pltpu.CompilerParams(
            collective_id=0, has_side_effects=True, vmem_limit_bytes=60 * 1024 * 1024
        ),
    )(
        velocity,
        wall_first,
        wall_second,
        jnp.asarray(even),
        jnp.asarray(odd),
        recycle_rows,
        weight_index,
        weight_table.reshape(1, -1),
    )
    accumulated_next = keep_rate * accumulated + step_size * tendency
    return (velocity + update_rate * accumulated_next, accumulated_next)


def solution(mesh):
    in_specs = (P(None, "gx", "ga", None), P(None, "gx", "ga", None), P(), P(), P(), P(), P())
    out_specs = (P(None, "gx", "ga", None), P(None, "gx", "ga", None))
    slabs, group = mesh.shape["gx"], mesh.shape["ga"]

    def body(velocity, *others):
        _, planes, rows, span = velocity.shape
        if planes == HALO == group and slabs > 3 and rows % 8 == 0 and span % 768 == 0:
            return fast_shards(slabs, group, velocity, *others)
        return shards(velocity, *others)

    return jax.shard_map(body, mesh=mesh, in_specs=in_specs, out_specs=out_specs, check_vma=False)
```
